512 devices in a mesh: cell: 16 (over x, z_hi), hour: 8 (over z_lo, core), cat: 4 (over y).
Axes of the slice: x: 4, y: 4, z: 16 (z_hi: 4, z_lo: 4; z = z_hi * 4 + z_lo), core: 2. Of those that a mesh axis runs over, the one named last changes fastest.
Arguments:
- demand: bfloat16 [512, 128, 16384], P('hour', 'cat', 'cell'), may hold values from -16 to 16
- hour_factor: bfloat16 [512, 64], P(('hour', 'cell')), may hold values from -1 to 1, as said below
- cat_factor: bfloat16 [128, 64], P(('cat', 'cell')), may hold values from -1 to 1, as said below
Outputs:
- cell_factor: float32 [64, 16384], P(None, 'cell')
The draws below stay inside these ranges and needn't reach their ends.
Inputs may be any that keep to these rules, and one draw needn't show every extreme that they name: `hour_factor`: factor entries; the largest magnitude is exactly 1. `cat_factor`: factor entries; the largest magnitude is exactly 1.
All inputs are finite; a program needn't handle non-finite values.
Results may differ from the reference program's by a relative error of at most 0.0029.
Values may be sent and summed in bfloat16 or wider, within the bound.
No kernel may reach another device: no remote copies, remote signals or barrier semaphores. Data moves between devices by JAX's collectives and lax.ppermute only.
A program may use at most 64 MiB of HBM per device.

```python
import math
import jax
import jax.numpy as jnp

R = 64
CATS = 128
CELLS = 16384
HOURS = 512


def factor_draw(key, count, width):
    first, second = jax.random.split(key)
    position = jnp.arange(count, dtype=jnp.float32)
    trend = 1.0 + 2.0 * position / (count - 1.0)
    spread = jnp.exp(jax.random.uniform(first, (count, 1), jnp.float32, 0.0, math.log(10.0)))
    base = jnp.clip(jax.random.normal(second, (count, width), jnp.float32), -3.0, 3.0)
    values = base * spread * trend[:, None]
    peak = jnp.max(jnp.abs(values))
    return (values / peak).astype(jnp.bfloat16)


def draw_hour_factor(key, part):
    return factor_draw(jax.random.fold_in(key, 11), HOURS, R)


def draw_cat_factor(key, part):
    return factor_draw(jax.random.fold_in(key, 23), CATS, R)


def raised(values, rng, source, target, parts, factor):
    owner, partner = [(jnp.arange(values.shape[dim]) // (values.shape[dim] // parts)).reshape([-1 if axis == dim else 1 for axis in range(values.ndim)]) for dim in (source, target)]
    chosen = jax.random.permutation(rng, parts)[partner]
    strong = (owner == chosen) | (owner == (partner + parts // 2) % parts)
    return jnp.where(strong, factor * values, values)


def steps_of(own_key, extent, cuts, smallest, largest):
    gain, own = 1.0, jax.random.fold_in(own_key, 6)
    for dim, parts in cuts:
        heights = jnp.exp(jax.random.uniform(jax.random.fold_in(own, dim), (parts,), jnp.float32, smallest / len(cuts), largest / len(cuts)))
        gain = gain * jnp.repeat(heights, extent[dim] // parts).reshape([-1 if axis == dim else 1 for axis in range(len(extent))])
    return gain


def gaussian_with(key, extent, deviation, bound, pieces, heavy, held_as=jnp.bfloat16):
    drawn = deviation * jax.random.normal(key, extent, jnp.float32)
    if pieces:
        drawn = drawn * steps_of(key, extent, pieces, -0.22, 0.18)
    return jnp.clip(raised(drawn, jax.random.fold_in(key, 3), *heavy), -bound, bound).astype(held_as)


def setup_inputs(seed: int = 0) -> dict:
    key_of = jax.random.split(jax.random.key(seed), 4)
    demand = gaussian_with(key_of[0], (HOURS, CATS, CELLS), 3.0, 16.0, ((0, 8), (1, 4), (2, 16)), (0, 2, 16, 2.0))
    hour_factor = draw_hour_factor(jax.random.fold_in(key_of[3], 71), 0)
    cat_factor = draw_cat_factor(jax.random.fold_in(key_of[3], 71), 0)
    return dict(demand=demand, hour_factor=hour_factor, cat_factor=cat_factor)


def reference(demand, hour_factor, cat_factor):
    hour_t = hour_factor.astype(jnp.float32).T
    cat_t = cat_factor.astype(jnp.float32).T
    khatri = (hour_t[:, :, None] * cat_t[:, None, :]).reshape(R, HOURS * CATS).astype(jnp.bfloat16)
    hour_gram = jnp.dot(hour_factor.T.astype(jnp.float32), hour_factor.astype(jnp.float32), preferred_element_type=jnp.float32)
    cat_gram = jnp.dot(cat_factor.T.astype(jnp.float32), cat_factor.astype(jnp.float32), preferred_element_type=jnp.float32)
    normal_matrix = hour_gram * cat_gram
    unfolded = demand.reshape(HOURS * CATS, CELLS)
    mttkrp = jnp.dot(khatri.astype(jnp.float32), unfolded.astype(jnp.float32), preferred_element_type=jnp.float32)
    lower_factor = jnp.linalg.cholesky(normal_matrix)
    return jax.scipy.linalg.cho_solve((lower_factor, True), mttkrp)
```

```python
import jax
import jax.numpy as jnp
from jax import lax
from jax.sharding import PartitionSpec as P

REST = ("hour", "cat")


def spread(block, axes, count):
    copies = jnp.broadcast_to(block[None], (count,) + block.shape)
    return lax.all_to_all(copies, axes, 0, 0)


def shards(demand, hour_factor, cat_factor, sizes):
    cell_n, hour_n, cat_n = sizes
    rest_n = hour_n * cat_n
    hour_own, rank = hour_factor.shape
    cat_own = cat_factor.shape[0]
    hours_here, cats_here, cells_here = demand.shape

    own = jnp.concatenate([hour_factor, cat_factor], axis=0)
    own = jnp.pad(own, ((0, 8 - hour_own - cat_own), (0, 128 - rank)))
    rows = spread(own, "cell", cell_n)
    hour_rows = rows[:, :hour_own, :rank].reshape(hours_here, rank)
    cat_rows = rows[:, hour_own : hour_own + cat_own, :rank].reshape(cats_here, rank)

    hour_t = hour_rows.astype(jnp.float32).T
    cat_t = cat_rows.astype(jnp.float32).T
    khatri = (
        (hour_t[:, :, None] * cat_t[:, None, :])
        .reshape(rank, hours_here * cats_here)
        .astype(jnp.bfloat16)
    )
    unfolded = demand.reshape(hours_here * cats_here, cells_here)
    partial = jnp.dot(khatri, unfolded, preferred_element_type=jnp.float32).astype(jnp.bfloat16)
    chunks = partial.reshape(4, 16, 8, 128).transpose(0, 2, 1, 3).reshape(rest_n, 16, 128)

    hour_share = lax.dynamic_slice_in_dim(hour_rows, lax.axis_index("cat") * (hours_here // cat_n), hours_here // cat_n)
    cat_share = lax.dynamic_slice_in_dim(cat_rows, lax.axis_index("hour") * (cats_here // hour_n), cats_here // hour_n)
    cat_share = jnp.pad(cat_share, ((0, 16 - cats_here // hour_n), (0, 0)))
    share = jnp.concatenate([hour_share, cat_share], axis=1)
    message = jnp.concatenate([chunks, jnp.broadcast_to(share[None], (rest_n, 16, 128))], axis=1)
    arrived = lax.all_to_all(message, REST, 0, 0)

    summed = arrived[:, :16].astype(jnp.float32).sum(0).astype(jnp.bfloat16)
    gathered = spread(summed, REST, rest_n)

    factors = arrived[:, 16:].reshape(rest_n * 16, 128)
    grams = jnp.dot(factors.T, factors, preferred_element_type=jnp.float32)
    normal_matrix = grams[:rank, :rank] * grams[rank:, rank:]
    lower_factor = jnp.linalg.cholesky(normal_matrix)

    mttkrp = gathered.reshape(4, 8, 16, 128).transpose(0, 2, 1, 3).reshape(rank, cells_here)
    return jax.scipy.linalg.cho_solve((lower_factor, True), mttkrp.astype(jnp.float32))


def solution(mesh):
    sizes = tuple(mesh.shape[axis] for axis in ("cell", "hour", "cat"))
    in_specs = (P("hour", "cat", "cell"), P(("hour", "cell"), None), P(("cat", "cell"), None))
    out_specs = P(None, "cell")

    def body(demand, hour_factor, cat_factor):
        return shards(demand, hour_factor, cat_factor, sizes)

    return jax.shard_map(body, mesh=mesh, in_specs=in_specs, out_specs=out_specs, check_vma=False)
```

```python
import functools

import jax
import jax.numpy as jnp
from jax import lax
from jax.experimental import pallas as pl
from jax.experimental.pallas import tpu as pltpu
from jax.sharding import PartitionSpec as P

REST = ("hour", "cat")
LANES = 128
GROUP = 8
TALL = 16
F32 = jnp.float32
BF16 = jnp.bfloat16


def iota(shape, dim):
    return lax.broadcasted_iota(jnp.int32, shape, dim)


def rows_kernel(hour_ref, cat_ref, out_ref):
    hour_own, rank = hour_ref.shape
    cat_own = cat_ref.shape[0]
    hours = hour_ref[...].astype(F32)
    cats = cat_ref[...].astype(F32)
    cats = jnp.concatenate([cats, jnp.zeros((hour_own - cat_own, rank), F32)], axis=0)
    own = jnp.concatenate([hours, cats], axis=1)
    own = jnp.concatenate([own, jnp.zeros((GROUP - hour_own, LANES), F32)], axis=0)
    out_ref[...] = jnp.broadcast_to(own.astype(BF16)[None], out_ref.shape)


def partial_kernel(rank, hour_own, cat_own, rows_ref, demand_ref, out_ref, groups_ref):
    cell_n = rows_ref.shape[0]
    hours_here, cats_here, cells_here = demand_ref.shape
    depth = hours_here * cats_here
    groups = rows_ref[...].astype(F32)
    groups_ref[...] = groups
    flat = groups.reshape(cell_n * GROUP, LANES)
    turned = flat.T.astype(BF16)
    column = iota((cell_n * GROUP, depth), 1)
    row = iota((cell_n * GROUP, depth), 0)
    hour = column // cats_here
    pick_hour = (row == (hour // hour_own) * GROUP + hour % hour_own).astype(F32).astype(BF16)
    cat = iota((cell_n * GROUP, LANES), 1) % cats_here
    cat_row = iota((cell_n * GROUP, LANES), 0)
    pick_cat = (cat_row == (cat // cat_own) * GROUP + cat % cat_own).astype(F32).astype(BF16)
    hour_cols = jnp.dot(turned[:rank], pick_hour, preferred_element_type=F32)
    cat_cols = jnp.dot(turned[rank:], pick_cat, preferred_element_type=F32)
    cat_cols = jnp.concatenate([cat_cols] * (depth // LANES), axis=1)
    khatri = (hour_cols * cat_cols).astype(BF16)

    width = 256
    across = cells_here // LANES
    for left in range(0, cells_here, width):
        block = demand_ref[:, :, left : left + width].reshape(depth, width)
        sums = jnp.dot(khatri, block, preferred_element_type=F32).astype(BF16)
        for down in range(rank // TALL):
            for over in range(width // LANES):
                out_ref[down * across + left // LANES + over, :TALL, :] = sums[
                    down * TALL : (down + 1) * TALL, over * LANES : (over + 1) * LANES
                ]

    hour_first = lax.axis_index("cat") * (TALL // hour_own)
    cat_groups = cats_here // lax.axis_size("hour") // cat_own
    cat_first = lax.axis_index("hour") * cat_groups
    left_half = iota((hour_own, LANES), 1) < rank
    pieces = []
    for step in range(TALL // hour_own):
        hours = groups_ref[hour_first + step][:hour_own]
        cats = groups_ref[cat_first + step][:hour_own] if step < cat_groups else jnp.zeros_like(hours)
        pieces.append(jnp.where(left_half, hours, cats))
    share = jnp.concatenate(pieces, axis=0).astype(BF16)
    out_ref[:, TALL:, :] = jnp.broadcast_to(share[None], (out_ref.shape[0], TALL, LANES))


def sum_kernel(arrived_ref, out_ref):
    count = arrived_ref.shape[0]
    terms = [arrived_ref[n, :TALL, :].astype(F32) for n in range(count)]
    while len(terms) > 1:
        terms = [terms[n] + terms[n + 1] for n in range(0, len(terms), 2)]
    out_ref[...] = jnp.broadcast_to(terms[0].astype(BF16)[None], out_ref.shape)


def inverse_kernel(rank, arrived_ref, out_ref):
    count = arrived_ref.shape[0]
    rows = arrived_ref[:, TALL:, :].reshape(count * TALL, LANES)
    grams = lax.dot_general(rows, rows, (((0,), (0,)), ((), ())), preferred_element_type=F32)
    normal = grams[:rank] * pltpu.roll(grams[rank:], rank, 1)
    row, lane = iota((rank, LANES), 0), iota((rank, LANES), 1)
    diagonal = jnp.where(row == lane, normal, 0.0)
    by_row = lax.rsqrt(jnp.sum(diagonal, axis=1, keepdims=True))
    mirrored = diagonal + pltpu.roll(diagonal, rank, 1)
    by_lane = lax.rsqrt(jnp.sum(mirrored, axis=0, keepdims=True))
    left_half = lane < rank
    work = jnp.where(left_half, normal * by_row * by_lane, (row + rank == lane).astype(F32))
    blocks = [work[n * 8 : (n + 1) * 8] for n in range(rank // 8)]
    sub = iota((8, LANES), 0)
    for first in range(0, rank, 2):
        home, at = first // 8, first % 8
        columns_a = [jnp.broadcast_to(b[:, first : first + 1], (8, LANES)) for b in blocks]
        columns_b = [jnp.broadcast_to(b[:, first + 1 : first + 2], (8, LANES)) for b in blocks]
        row_a, row_b = blocks[home][at : at + 1], blocks[home][at + 1 : at + 2]
        p_aa, p_ba = columns_a[home][at : at + 1], columns_a[home][at + 1 : at + 2]
        p_ab, p_bb = columns_b[home][at : at + 1], columns_b[home][at + 1 : at + 2]
        scale = 1.0 / (p_aa * p_bb - p_ab * p_ba)
        new_a = (p_bb * row_a - p_ab * row_b) * scale
        new_b = (p_aa * row_b - p_ba * row_a) * scale
        new_a, new_b = jnp.broadcast_to(new_a, (8, LANES)), jnp.broadcast_to(new_b, (8, LANES))
        blocks = [b - (ca * new_a + cb * new_b) for b, ca, cb in zip(blocks, columns_a, columns_b)]
        blocks[home] = jnp.where(sub == at, new_a, jnp.where(sub == at + 1, new_b, blocks[home]))
    inverse = jnp.concatenate(blocks, axis=0) * by_row * by_lane
    inverse = pltpu.roll(inverse, rank, 1)
    high = inverse.astype(BF16)
    rest = inverse - high.astype(F32)
    middle = rest.astype(BF16)
    low = (rest - middle.astype(F32)).astype(BF16)
    out_ref[:rank] = high
    out_ref[rank : 2 * rank] = middle
    out_ref[2 * rank :] = low


def solve_kernel(rank, inverse_ref, sums_ref, out_ref):
    cells_here = out_ref.shape[1]
    across = cells_here // LANES
    lhs = inverse_ref[...][:, :rank]
    for over in range(0, across, 2):
        rhs = jnp.concatenate(
            [
                jnp.concatenate([sums_ref[down * across + over + n] for down in range(rank // TALL)], axis=0)
                for n in range(2)
            ],
            axis=1,
        )
        terms = jnp.dot(lhs, rhs, preferred_element_type=F32)
        out_ref[:, over * LANES : (over + 2) * LANES] = terms[:rank] + (
            terms[rank : 2 * rank] + terms[2 * rank :]
        )


def call(kernel, shape, dtype, operands, flops, moved, scratch=()):
    vmem = pl.BlockSpec(memory_space=pltpu.VMEM)
    return pl.pallas_call(
        kernel,
        out_shape=jax.ShapeDtypeStruct(shape, dtype),
        in_specs=[vmem] * len(operands),
        out_specs=vmem,
        scratch_shapes=list(scratch),
        compiler_params=pltpu.CompilerParams(vmem_limit_bytes=24 * 1024 * 1024),
        cost_estimate=pl.CostEstimate(flops=flops, bytes_accessed=moved, transcendentals=0),
    )(*operands)


def shards(demand, hour_factor, cat_factor, sizes):
    cell_n, hour_n, cat_n = sizes
    rest_n = hour_n * cat_n
    hour_own, rank = hour_factor.shape
    cat_own = cat_factor.shape[0]
    cells_here = demand.shape[2]

    own = call(rows_kernel, (cell_n, GROUP, LANES), BF16, (hour_factor, cat_factor), 1000, 40000)
    rows = lax.all_to_all(own, "cell", 0, 0)
    message = call(
        functools.partial(partial_kernel, rank, hour_own, cat_own),
        (rest_n, 2 * TALL, LANES),
        BF16,
        (rows, demand),
        2 * rank * demand.size,
        2 * demand.size,
        [pltpu.VMEM((cell_n, GROUP, LANES), F32)],
    )
    arrived = lax.all_to_all(message, REST, 0, 0)
    summed = call(sum_kernel, (rest_n, TALL, LANES), BF16, (arrived,), 100000, 400000)
    gathered = lax.all_to_all(summed, REST, 0, 0)
    inverse = call(
        functools.partial(inverse_kernel, rank), (3 * rank, LANES), BF16, (arrived,), 2**24, 10**7
    )
    return call(
        functools.partial(solve_kernel, rank),
        (rank, cells_here),
        F32,
        (inverse, gathered),
        6 * rank * rank * cells_here,
        400000,
    )


def solution(mesh):
    sizes = tuple(mesh.shape[axis] for axis in ("cell", "hour", "cat"))
    in_specs = (P("hour", "cat", "cell"), P(("hour", "cell"), None), P(("cat", "cell"), None))
    out_specs = P(None, "cell")

    def body(demand, hour_factor, cat_factor):
        return shards(demand, hour_factor, cat_factor, sizes)

    return jax.shard_map(body, mesh=mesh, in_specs=in_specs, out_specs=out_specs, check_vma=False)
```

```python
import functools

import jax
import jax.numpy as jnp
from jax import lax
from jax.experimental import pallas as pl
from jax.experimental.pallas import tpu as pltpu
from jax.sharding import PartitionSpec as P

REST = ("hour", "cat")
LANES = 128
GROUP = 8
TALL = 16
F32 = jnp.float32
BF16 = jnp.bfloat16
STRIP = 8


def iota(shape, dim):
    return lax.broadcasted_iota(jnp.int32, shape, dim)


def rows_kernel(own_ref, out_ref):
    out_ref[...] = jnp.broadcast_to(own_ref[...][None], out_ref.shape)


def partial_kernel(rank, hour_own, cat_own, rows_ref, demand_in, out_ref, groups_ref, demand_ref, sems):
    width = 256
    copies = []
    for n in range(demand_in.shape[0] // STRIP):
        part = pl.ds(n * STRIP, STRIP)
        copies.append(pltpu.make_async_copy(demand_in.at[part], demand_ref.at[part], sems.at[n]))
        copies[-1].start()
    cell_n = rows_ref.shape[0]
    hours_here, cats_here, cells_here = demand_ref.shape
    depth = hours_here * cats_here
    groups = rows_ref[...].astype(F32)
    groups_ref[...] = groups
    flat = groups.reshape(cell_n * GROUP, LANES)
    turned = flat.T.astype(BF16)
    column = iota((cell_n * GROUP, depth), 1)
    row = iota((cell_n * GROUP, depth), 0)
    hour = column // cats_here
    pick_hour = (row == (hour // hour_own) * GROUP + hour % hour_own).astype(F32).astype(BF16)
    cat = iota((cell_n * GROUP, LANES), 1) % cats_here
    cat_row = iota((cell_n * GROUP, LANES), 0)
    pick_cat = (cat_row == (cat // cat_own) * GROUP + cat % cat_own).astype(F32).astype(BF16)
    hour_cols = jnp.dot(turned[:rank], pick_hour, preferred_element_type=F32)
    cat_cols = jnp.dot(turned[rank:], pick_cat, preferred_element_type=F32)
    cat_cols = jnp.concatenate([cat_cols] * (depth // LANES), axis=1)
    khatri = (hour_cols * cat_cols).astype(BF16)

    hour_first = lax.axis_index("cat") * (TALL // hour_own)
    cat_groups = cats_here // lax.axis_size("hour") // cat_own
    cat_first = lax.axis_index("hour") * cat_groups
    left_half = iota((hour_own, LANES), 1) < rank
    pieces = []
    for step in range(TALL // hour_own):
        hours = groups_ref[hour_first + step][:hour_own]
        cats = groups_ref[cat_first + step][:hour_own] if step < cat_groups else jnp.zeros_like(hours)
        pieces.append(jnp.where(left_half, hours, cats))
    share = jnp.concatenate(pieces, axis=0).astype(BF16)
    out_ref[:, TALL:, :] = jnp.broadcast_to(share[None], (out_ref.shape[0], TALL, LANES))

    across = cells_here // LANES
    chunk = STRIP * cats_here
    totals = [0.0] * (cells_here // width)
    for n, copy in enumerate(copies):
        copy.wait()
        columns = khatri[:, n * chunk : (n + 1) * chunk]
        for strip in range(len(totals)):
            block = demand_ref[n * STRIP : (n + 1) * STRIP, :, strip * width : (strip + 1) * width]
            totals[strip] += jnp.dot(columns, block.reshape(chunk, width), preferred_element_type=F32)
    for strip, total in enumerate(totals):
        left, sums = strip * width, total.astype(BF16)
        for down in range(rank // TALL):
            for over in range(width // LANES):
                out_ref[down * across + left // LANES + over, :TALL, :] = sums[
                    down * TALL : (down + 1) * TALL, over * LANES : (over + 1) * LANES
                ]


def sum_kernel(arrived_ref, out_ref):
    count = arrived_ref.shape[0]
    terms = [arrived_ref[n, :TALL, :].astype(F32) for n in range(count)]
    while len(terms) > 1:
        terms = [terms[n] + terms[n + 1] for n in range(0, len(terms), 2)]
    out_ref[...] = jnp.broadcast_to(terms[0].astype(BF16)[None], out_ref.shape)


def inverse_kernel(rank, arrived_ref, out_ref):
    count = arrived_ref.shape[0]
    rows = arrived_ref[:, TALL:, :].reshape(count * TALL, LANES)
    grams = lax.dot_general(rows, rows, (((0,), (0,)), ((), ())), preferred_element_type=F32)
    normal = grams[:rank] * pltpu.roll(grams[rank:], rank, 1)
    row, lane = iota((rank, LANES), 0), iota((rank, LANES), 1)
    diagonal = jnp.where(row == lane, normal, 0.0)
    by_row = lax.rsqrt(jnp.sum(diagonal, axis=1, keepdims=True))
    mirrored = diagonal + pltpu.roll(diagonal, rank, 1)
    by_lane = lax.rsqrt(jnp.sum(mirrored, axis=0, keepdims=True))
    left_half = lane < rank
    work = jnp.where(left_half, normal * by_row * by_lane, (row + rank == lane).astype(F32))
    blocks = [work[n * 8 : (n + 1) * 8] for n in range(rank // 8)]
    sub = iota((8, LANES), 0)
    for first in range(0, rank, 2):
        home, at = first // 8, first % 8
        columns_a = [jnp.broadcast_to(b[:, first : first + 1], (8, LANES)) for b in blocks]
        columns_b = [jnp.broadcast_to(b[:, first + 1 : first + 2], (8, LANES)) for b in blocks]
        row_a, row_b = blocks[home][at : at + 1], blocks[home][at + 1 : at + 2]
        p_aa, p_ba = columns_a[home][at : at + 1], columns_a[home][at + 1 : at + 2]
        p_ab, p_bb = columns_b[home][at : at + 1], columns_b[home][at + 1 : at + 2]
        scale = 1.0 / (p_aa * p_bb - p_ab * p_ba)
        new_a = (p_bb * row_a - p_ab * row_b) * scale
        new_b = (p_aa * row_b - p_ba * row_a) * scale
        new_a, new_b = jnp.broadcast_to(new_a, (8, LANES)), jnp.broadcast_to(new_b, (8, LANES))
        blocks = [b - (ca * new_a + cb * new_b) for b, ca, cb in zip(blocks, columns_a, columns_b)]
        blocks[home] = jnp.where(sub == at, new_a, jnp.where(sub == at + 1, new_b, blocks[home]))
    inverse = jnp.concatenate(blocks, axis=0) * by_row * by_lane
    inverse = pltpu.roll(inverse, rank, 1)
    high = inverse.astype(BF16)
    rest = inverse - high.astype(F32)
    middle = rest.astype(BF16)
    low = (rest - middle.astype(F32)).astype(BF16)
    out_ref[:rank] = high
    out_ref[rank : 2 * rank] = middle
    out_ref[2 * rank :] = low


def solve_kernel(rank, inverse_ref, sums_ref, out_hbm, out_ref, sems):
    copies = []
    cells_here = out_ref.shape[1]
    across = cells_here // LANES
    lhs = inverse_ref[...][:, :rank]
    for over in range(0, across, 2):
        rhs = jnp.concatenate(
            [
                jnp.concatenate([sums_ref[down * across + over + n] for down in range(rank // TALL)], axis=0)
                for n in range(2)
            ],
            axis=1,
        )
        terms = jnp.dot(lhs, rhs, preferred_element_type=F32)
        out_ref[:, over * LANES : (over + 2) * LANES] = terms[:rank] + (
            terms[rank : 2 * rank] + terms[2 * rank :]
        )
        part = pl.ds(over * LANES, 2 * LANES)
        copies.append(pltpu.make_async_copy(out_ref.at[:, part], out_hbm.at[:, part], sems.at[over // 2]))
        copies[-1].start()
    for copy in copies:
        copy.wait()


def call(kernel, shape, dtype, operands, flops, moved, scratch=(), left=(), leave_out=False, mib=24):
    vmem, anywhere = pl.BlockSpec(memory_space=pltpu.VMEM), pl.BlockSpec(memory_space=pltpu.HBM)
    return pl.pallas_call(
        kernel,
        out_shape=jax.ShapeDtypeStruct(shape, dtype),
        in_specs=[anywhere if n in left else vmem for n in range(len(operands))],
        out_specs=anywhere if leave_out else vmem,
        scratch_shapes=list(scratch),
        compiler_params=pltpu.CompilerParams(vmem_limit_bytes=mib * 1024 * 1024),
        cost_estimate=pl.CostEstimate(flops=flops, bytes_accessed=moved, transcendentals=0),
    )(*operands)


def shards(demand, hour_factor, cat_factor, sizes):
    cell_n, hour_n, cat_n = sizes
    rest_n = hour_n * cat_n
    hour_own, rank = hour_factor.shape
    cat_own = cat_factor.shape[0]
    cells_here = demand.shape[2]

    own = jnp.concatenate(
        [
            jnp.pad(hour_factor, ((0, GROUP - hour_own), (0, 0))),
            jnp.pad(cat_factor, ((0, GROUP - cat_own), (0, 0))),
        ],
        axis=1,
    )
    own = call(rows_kernel, (cell_n, GROUP, LANES), BF16, (own,), 1000, 40000)
    rows = lax.all_to_all(own, "cell", 0, 0)
    message = call(
        functools.partial(partial_kernel, rank, hour_own, cat_own),
        (rest_n, 2 * TALL, LANES),
        BF16,
        (rows, demand),
        2 * rank * demand.size,
        2 * demand.size,
        [
            pltpu.VMEM((cell_n, GROUP, LANES), F32),
            pltpu.VMEM(demand.shape, BF16),
            pltpu.SemaphoreType.DMA((demand.shape[0] // STRIP,)),
        ],
        (1,),
        mib=50,
    )
    arrived = lax.all_to_all(message, REST, 0, 0)
    summed = call(sum_kernel, (rest_n, TALL, LANES), BF16, (arrived,), 100000, 400000)
    gathered = lax.all_to_all(summed, REST, 0, 0)
    inverse = call(
        functools.partial(inverse_kernel, rank), (3 * rank, LANES), BF16, (arrived,), 2**24, 10**7
    )
    return call(
        functools.partial(solve_kernel, rank),
        (rank, cells_here),
        F32,
        (inverse, gathered),
        6 * rank * rank * cells_here,
        400000,
        [pltpu.VMEM((rank, cells_here), F32), pltpu.SemaphoreType.DMA((cells_here // LANES // 2,))],
        (),
        True,
    )


def solution(mesh):
    sizes = tuple(mesh.shape[axis] for axis in ("cell", "hour", "cat"))
    in_specs = (P("hour", "cat", "cell"), P(("hour", "cell"), None), P(("cat", "cell"), None))
    out_specs = P(None, "cell")

    def body(demand, hour_factor, cat_factor):
        return shards(demand, hour_factor, cat_factor, sizes)

    return jax.shard_map(body, mesh=mesh, in_specs=in_specs, out_specs=out_specs, check_vma=False)
```

```python
import functools

import jax
import jax.numpy as jnp
from jax import lax
from jax.experimental import pallas as pl
from jax.experimental.pallas import tpu as pltpu
from jax.sharding import PartitionSpec as P

REST = ("hour", "cat")
LANES = 128
GROUP = 8
TALL = 16
F32 = jnp.float32
BF16 = jnp.bfloat16
CELL_FIRST = 10
REST_FIRST = 22
STRIP = 8


def iota(shape, dim):
    return lax.broadcasted_iota(jnp.int32, shape, dim)


def exchange(blocks, axes, first):
    order = [n ^ first for n in range(blocks.shape[0])]
    return lax.all_to_all(blocks, axes, 0, 0, axis_index_groups=[order])


def rows_kernel(own_ref, out_ref):
    out_ref[...] = jnp.broadcast_to(own_ref[...][None], out_ref.shape)


def partial_kernel(rank, hour_own, cat_own, rows_ref, demand_in, out_ref, groups_ref, demand_ref, sems):
    width = 256
    copies = []
    for n in range(demand_in.shape[0] // STRIP):
        part = pl.ds(n * STRIP, STRIP)
        copies.append(pltpu.make_async_copy(demand_in.at[part], demand_ref.at[part], sems.at[n]))
        copies[-1].start()
    cell_n = rows_ref.shape[0]
    hours_here, cats_here, cells_here = demand_ref.shape
    depth = hours_here * cats_here
    groups = rows_ref[...].astype(F32)
    groups_ref[...] = groups
    flat = groups.reshape(cell_n * GROUP, LANES)
    turned = flat.T.astype(BF16)
    column = iota((cell_n * GROUP, depth), 1)
    row = iota((cell_n * GROUP, depth), 0)
    hour = column // cats_here
    pick_hour = (row == ((hour // hour_own) ^ CELL_FIRST) * GROUP + hour % hour_own).astype(F32).astype(BF16)
    cat = iota((cell_n * GROUP, LANES), 1) % cats_here
    cat_row = iota((cell_n * GROUP, LANES), 0)
    pick_cat = (cat_row == ((cat // cat_own) ^ CELL_FIRST) * GROUP + cat % cat_own).astype(F32).astype(BF16)
    hour_cols = jnp.dot(turned[:rank], pick_hour, preferred_element_type=F32)
    cat_cols = jnp.dot(turned[rank:], pick_cat, preferred_element_type=F32)
    cat_cols = jnp.concatenate([cat_cols] * (depth // LANES), axis=1)
    khatri = (hour_cols * cat_cols).astype(BF16)

    hour_first = lax.axis_index("cat") * (TALL // hour_own)
    cat_groups = cats_here // lax.axis_size("hour") // cat_own
    cat_first = lax.axis_index("hour") * cat_groups
    left_half = iota((hour_own, LANES), 1) < rank
    pieces = []
    for step in range(TALL // hour_own):
        hours = groups_ref[hour_first + step][:hour_own]
        cats = groups_ref[cat_first + step][:hour_own] if step < cat_groups else jnp.zeros_like(hours)
        pieces.append(jnp.where(left_half, hours, cats))
    share = jnp.concatenate(pieces, axis=0).astype(BF16)
    out_ref[:, TALL:, :] = jnp.broadcast_to(share[None], (out_ref.shape[0], TALL, LANES))

    across = cells_here // LANES
    chunk = STRIP * cats_here
    totals = [0.0] * (cells_here // width)
    for n, copy in enumerate(copies):
        copy.wait()
        columns = khatri[:, n * chunk : (n + 1) * chunk]
        for strip in range(len(totals)):
            block = demand_ref[n * STRIP : (n + 1) * STRIP, :, strip * width : (strip + 1) * width]
            totals[strip] += jnp.dot(columns, block.reshape(chunk, width), preferred_element_type=F32)
    for strip, total in enumerate(totals):
        left, sums = strip * width, total.astype(BF16)
        for down in range(rank // TALL):
            for over in range(width // LANES):
                out_ref[down * across + left // LANES + over, :TALL, :] = sums[
                    down * TALL : (down + 1) * TALL, over * LANES : (over + 1) * LANES
                ]


def sum_kernel(arrived_ref, out_ref):
    count = arrived_ref.shape[0]
    terms = [arrived_ref[n, :TALL, :].astype(F32) for n in range(count)]
    while len(terms) > 1:
        terms = [terms[n] + terms[n + 1] for n in range(0, len(terms), 2)]
    out_ref[...] = jnp.broadcast_to(terms[0].astype(BF16)[None], out_ref.shape)


def inverse_kernel(rank, arrived_ref, out_ref):
    count = arrived_ref.shape[0]
    rows = arrived_ref[:, TALL:, :].reshape(count * TALL, LANES)
    grams = lax.dot_general(rows, rows, (((0,), (0,)), ((), ())), preferred_element_type=F32)
    normal = grams[:rank] * pltpu.roll(grams[rank:], rank, 1)
    row, lane = iota((rank, LANES), 0), iota((rank, LANES), 1)
    diagonal = jnp.where(row == lane, normal, 0.0)
    by_row = lax.rsqrt(jnp.sum(diagonal, axis=1, keepdims=True))
    mirrored = diagonal + pltpu.roll(diagonal, rank, 1)
    by_lane = lax.rsqrt(jnp.sum(mirrored, axis=0, keepdims=True))
    left_half = lane < rank
    work = jnp.where(left_half, normal * by_row * by_lane, (row + rank == lane).astype(F32))
    blocks = [work[n * 8 : (n + 1) * 8] for n in range(rank // 8)]
    sub = iota((8, LANES), 0)
    for first in range(0, rank, 2):
        home, at = first // 8, first % 8
        columns_a = [jnp.broadcast_to(b[:, first : first + 1], (8, LANES)) for b in blocks]
        columns_b = [jnp.broadcast_to(b[:, first + 1 : first + 2], (8, LANES)) for b in blocks]
        row_a, row_b = blocks[home][at : at + 1], blocks[home][at + 1 : at + 2]
        p_aa, p_ba = columns_a[home][at : at + 1], columns_a[home][at + 1 : at + 2]
        p_ab, p_bb = columns_b[home][at : at + 1], columns_b[home][at + 1 : at + 2]
        scale = 1.0 / (p_aa * p_bb - p_ab * p_ba)
        new_a = (p_bb * row_a - p_ab * row_b) * scale
        new_b = (p_aa * row_b - p_ba * row_a) * scale
        new_a, new_b = jnp.broadcast_to(new_a, (8, LANES)), jnp.broadcast_to(new_b, (8, LANES))
        blocks = [b - (ca * new_a + cb * new_b) for b, ca, cb in zip(blocks, columns_a, columns_b)]
        blocks[home] = jnp.where(sub == at, new_a, jnp.where(sub == at + 1, new_b, blocks[home]))
    inverse = jnp.concatenate(blocks, axis=0) * by_row * by_lane
    inverse = pltpu.roll(inverse, rank, 1)
    high = inverse.astype(BF16)
    rest = inverse - high.astype(F32)
    middle = rest.astype(BF16)
    low = (rest - middle.astype(F32)).astype(BF16)
    out_ref[:rank] = high
    out_ref[rank : 2 * rank] = middle
    out_ref[2 * rank :] = low


def solve_kernel(rank, inverse_ref, sums_ref, out_hbm, out_ref, sems):
    copies = []
    cells_here = out_ref.shape[1]
    across = cells_here // LANES
    lhs = inverse_ref[...][:, :rank]
    for over in range(0, across, 2):
        rhs = jnp.concatenate(
            [
                jnp.concatenate([sums_ref[down * across + over + n] for down in range(rank // TALL)], axis=0)
                for n in range(2)
            ],
            axis=1,
        )
        terms = jnp.dot(lhs, rhs, preferred_element_type=F32)
        out_ref[:, over * LANES : (over + 2) * LANES] = terms[:rank] + (
            terms[rank : 2 * rank] + terms[2 * rank :]
        )
        part = pl.ds(over * LANES, 2 * LANES)
        copies.append(pltpu.make_async_copy(out_ref.at[:, part], out_hbm.at[:, part], sems.at[over // 2]))
        copies[-1].start()
    for copy in copies:
        copy.wait()


def call(kernel, shape, dtype, operands, flops, moved, scratch=(), left=(), leave_out=False, mib=24):
    vmem, anywhere = pl.BlockSpec(memory_space=pltpu.VMEM), pl.BlockSpec(memory_space=pltpu.HBM)
    return pl.pallas_call(
        kernel,
        out_shape=jax.ShapeDtypeStruct(shape, dtype),
        in_specs=[anywhere if n in left else vmem for n in range(len(operands))],
        out_specs=anywhere if leave_out else vmem,
        scratch_shapes=list(scratch),
        compiler_params=pltpu.CompilerParams(vmem_limit_bytes=mib * 1024 * 1024),
        cost_estimate=pl.CostEstimate(flops=flops, bytes_accessed=moved, transcendentals=0),
    )(*operands)


def shards(demand, hour_factor, cat_factor, sizes):
    cell_n, hour_n, cat_n = sizes
    rest_n = hour_n * cat_n
    hour_own, rank = hour_factor.shape
    cat_own = cat_factor.shape[0]
    cells_here = demand.shape[2]

    own = jnp.concatenate(
        [
            jnp.pad(hour_factor, ((0, GROUP - hour_own), (0, 0))),
            jnp.pad(cat_factor, ((0, GROUP - cat_own), (0, 0))),
        ],
        axis=1,
    )
    own = call(rows_kernel, (cell_n, GROUP, LANES), BF16, (own,), 1000, 40000)
    rows = exchange(own, "cell", CELL_FIRST)
    message = call(
        functools.partial(partial_kernel, rank, hour_own, cat_own),
        (rest_n, 2 * TALL, LANES),
        BF16,
        (rows, demand),
        2 * rank * demand.size,
        2 * demand.size,
        [
            pltpu.VMEM((cell_n, GROUP, LANES), F32),
            pltpu.VMEM(demand.shape, BF16),
            pltpu.SemaphoreType.DMA((demand.shape[0] // STRIP,)),
        ],
        (1,),
        mib=50,
    )
    arrived = exchange(message, REST, REST_FIRST)
    summed = call(sum_kernel, (rest_n, TALL, LANES), BF16, (arrived,), 100000, 400000)
    gathered = exchange(summed, REST, REST_FIRST)
    inverse = call(
        functools.partial(inverse_kernel, rank), (3 * rank, LANES), BF16, (arrived,), 2**24, 10**7
    )
    return call(
        functools.partial(solve_kernel, rank),
        (rank, cells_here),
        F32,
        (inverse, gathered),
        6 * rank * rank * cells_here,
        400000,
        [pltpu.VMEM((rank, cells_here), F32), pltpu.SemaphoreType.DMA((cells_here // LANES // 2,))],
        (),
        True,
    )


def solution(mesh):
    sizes = tuple(mesh.shape[axis] for axis in ("cell", "hour", "cat"))
    in_specs = (P("hour", "cat", "cell"), P(("hour", "cell"), None), P(("cat", "cell"), None))
    out_specs = P(None, "cell")

    def body(demand, hour_factor, cat_factor):
        return shards(demand, hour_factor, cat_factor, sizes)

    return jax.shard_map(body, mesh=mesh, in_specs=in_specs, out_specs=out_specs, check_vma=False)
```

```python
import functools

import jax
import jax.numpy as jnp
from jax import lax
from jax.experimental import pallas as pl
from jax.experimental.pallas import tpu as pltpu
from jax.sharding import PartitionSpec as P

REST = ("hour", "cat")
LANES = 128
GROUP = 8
TALL = 16
SUMS = 8
HOURS = 4
F32 = jnp.float32
BF16 = jnp.bfloat16
CELL_FIRST = 10
REST_FIRST = 22
STRIP = 8


def iota(shape, dim):
    return lax.broadcasted_iota(jnp.int32, shape, dim)


def exchange(blocks, axes, first):
    order = [n ^ first for n in range(blocks.shape[0])]
    return lax.all_to_all(blocks, axes, 0, 0, axis_index_groups=[order])


def rows_kernel(own_ref, out_ref):
    out_ref[...] = jnp.broadcast_to(own_ref[...][None], out_ref.shape)


def partial_kernel(rank, hour_own, cat_own, rows_ref, demand_in, out_ref, groups_ref, demand_ref, sems):
    width = 256
    copies = []
    for n in range(demand_in.shape[0] // STRIP):
        part = pl.ds(n * STRIP, STRIP)
        copies.append(pltpu.make_async_copy(demand_in.at[part], demand_ref.at[part], sems.at[n]))
        copies[-1].start()
    cell_n = rows_ref.shape[0]
    hours_here, cats_here, cells_here = demand_ref.shape
    depth = hours_here * cats_here
    groups = rows_ref[...].astype(F32)
    groups_ref[...] = groups
    flat = groups.reshape(cell_n * GROUP, LANES)
    turned = flat.T.astype(BF16)
    column = iota((cell_n * GROUP, depth), 1)
    row = iota((cell_n * GROUP, depth), 0)
    hour = column // cats_here
    pick_hour = (row == ((hour // hour_own) ^ CELL_FIRST) * GROUP + hour % hour_own).astype(F32).astype(BF16)
    cat = iota((cell_n * GROUP, LANES), 1) % cats_here
    cat_row = iota((cell_n * GROUP, LANES), 0)
    pick_cat = (cat_row == ((cat // cat_own) ^ CELL_FIRST) * GROUP + cat % cat_own).astype(F32).astype(BF16)
    hour_cols = jnp.dot(turned[:rank], pick_hour, preferred_element_type=F32)
    cat_cols = jnp.dot(turned[rank:], pick_cat, preferred_element_type=F32)
    cat_cols = jnp.concatenate([cat_cols] * (depth // LANES), axis=1)
    khatri = (hour_cols * cat_cols).astype(BF16)

    left_half = iota((GROUP, LANES), 1) < rank
    hour_first = lax.axis_index("cat") * (TALL // hour_own)
    hours = [groups_ref[hour_first + step][:hour_own] for step in range(TALL // hour_own)]
    over = jnp.concatenate(hours[:2], axis=0)
    under = jnp.concatenate(hours[2:], axis=0)
    share = jnp.where(left_half, over, pltpu.roll(under, rank, 1)).astype(BF16)
    out_ref[:, SUMS : SUMS + HOURS] = jnp.broadcast_to(
        share.reshape(1, HOURS, 2, LANES), (out_ref.shape[0], HOURS, 2, LANES)
    )
    cat_first = lax.axis_index("hour") * 2
    over, under = groups_ref[cat_first], groups_ref[cat_first + 1]
    share = jnp.where(left_half, pltpu.roll(over, rank, 1), under)[:cat_own].astype(BF16)
    out_ref[:, SUMS + HOURS] = jnp.broadcast_to(share[None], (out_ref.shape[0], 2, LANES))

    across = cells_here // LANES
    chunk = STRIP * cats_here
    totals = [0.0] * (cells_here // width)
    for n, copy in enumerate(copies):
        copy.wait()
        columns = khatri[:, n * chunk : (n + 1) * chunk]
        for strip in range(len(totals)):
            block = demand_ref[n * STRIP : (n + 1) * STRIP, :, strip * width : (strip + 1) * width]
            totals[strip] += jnp.dot(columns, block.reshape(chunk, width), preferred_element_type=F32)
    for strip, total in enumerate(totals):
        left, sums = strip * width, total.astype(BF16)
        for down in range(rank // TALL):
            for over in range(width // LANES):
                piece = sums[down * TALL : (down + 1) * TALL, over * LANES : (over + 1) * LANES]
                out_ref[down * across + left // LANES + over, :SUMS] = piece.reshape(SUMS, 2, LANES)


def sum_kernel(arrived_ref, out_ref):
    count = arrived_ref.shape[0]
    terms = [arrived_ref[n, :SUMS].astype(F32) for n in range(count)]
    while len(terms) > 1:
        terms = [terms[n] + terms[n + 1] for n in range(0, len(terms), 2)]
    out_ref[...] = jnp.broadcast_to(terms[0].reshape(TALL, LANES).astype(BF16)[None], out_ref.shape)


def gram(pairs, rank):
    rows = pairs.astype(F32).reshape(-1, LANES).astype(BF16)
    both = lax.dot_general(rows, rows, (((0,), (0,)), ((), ())), preferred_element_type=F32)
    return both[:rank] + pltpu.roll(both[rank:], rank, 1)


def inverse_kernel(rank, arrived_ref, out_ref):
    normal = gram(arrived_ref[:, SUMS : SUMS + HOURS], rank) * gram(arrived_ref[:, SUMS + HOURS], rank)
    row, lane = iota((rank, LANES), 0), iota((rank, LANES), 1)
    diagonal = jnp.where(row == lane, normal, 0.0)
    by_row = lax.rsqrt(jnp.sum(diagonal, axis=1, keepdims=True))
    mirrored = diagonal + pltpu.roll(diagonal, rank, 1)
    by_lane = lax.rsqrt(jnp.sum(mirrored, axis=0, keepdims=True))
    left_half = lane < rank
    work = jnp.where(left_half, normal * by_row * by_lane, (row + rank == lane).astype(F32))
    blocks = [work[n * 8 : (n + 1) * 8] for n in range(rank // 8)]
    sub = iota((8, LANES), 0)
    for first in range(0, rank, 2):
        home, at = first // 8, first % 8
        columns_a = [jnp.broadcast_to(b[:, first : first + 1], (8, LANES)) for b in blocks]
        columns_b = [jnp.broadcast_to(b[:, first + 1 : first + 2], (8, LANES)) for b in blocks]
        row_a, row_b = blocks[home][at : at + 1], blocks[home][at + 1 : at + 2]
        p_aa, p_ba = columns_a[home][at : at + 1], columns_a[home][at + 1 : at + 2]
        p_ab, p_bb = columns_b[home][at : at + 1], columns_b[home][at + 1 : at + 2]
        scale = 1.0 / (p_aa * p_bb - p_ab * p_ba)
        new_a = (p_bb * row_a - p_ab * row_b) * scale
        new_b = (p_aa * row_b - p_ba * row_a) * scale
        new_a, new_b = jnp.broadcast_to(new_a, (8, LANES)), jnp.broadcast_to(new_b, (8, LANES))
        blocks = [b - (ca * new_a + cb * new_b) for b, ca, cb in zip(blocks, columns_a, columns_b)]
        blocks[home] = jnp.where(sub == at, new_a, jnp.where(sub == at + 1, new_b, blocks[home]))
    inverse = jnp.concatenate(blocks, axis=0) * by_row * by_lane
    inverse = pltpu.roll(inverse, rank, 1)
    high = inverse.astype(BF16)
    rest = inverse - high.astype(F32)
    middle = rest.astype(BF16)
    low = (rest - middle.astype(F32)).astype(BF16)
    out_ref[:rank] = high
    out_ref[rank : 2 * rank] = middle
    out_ref[2 * rank :] = low


def solve_kernel(rank, inverse_ref, sums_ref, out_hbm, out_ref, sems):
    copies = []
    cells_here = out_ref.shape[1]
    across = cells_here // LANES
    lhs = inverse_ref[...][:, :rank]
    for over in range(0, across, 2):
        rhs = jnp.concatenate(
            [
                jnp.concatenate([sums_ref[down * across + over + n] for down in range(rank // TALL)], axis=0)
                for n in range(2)
            ],
            axis=1,
        )
        terms = jnp.dot(lhs, rhs, preferred_element_type=F32)
        out_ref[:, over * LANES : (over + 2) * LANES] = terms[:rank] + (
            terms[rank : 2 * rank] + terms[2 * rank :]
        )
        part = pl.ds(over * LANES, 2 * LANES)
        copies.append(pltpu.make_async_copy(out_ref.at[:, part], out_hbm.at[:, part], sems.at[over // 2]))
        copies[-1].start()
    for copy in copies:
        copy.wait()


def call(kernel, shape, dtype, operands, flops, moved, scratch=(), left=(), leave_out=False, mib=24):
    vmem, anywhere = pl.BlockSpec(memory_space=pltpu.VMEM), pl.BlockSpec(memory_space=pltpu.HBM)
    return pl.pallas_call(
        kernel,
        out_shape=jax.ShapeDtypeStruct(shape, dtype),
        in_specs=[anywhere if n in left else vmem for n in range(len(operands))],
        out_specs=anywhere if leave_out else vmem,
        scratch_shapes=list(scratch),
        compiler_params=pltpu.CompilerParams(vmem_limit_bytes=mib * 1024 * 1024),
        cost_estimate=pl.CostEstimate(flops=flops, bytes_accessed=moved, transcendentals=0),
    )(*operands)


def shards(demand, hour_factor, cat_factor, sizes):
    cell_n, hour_n, cat_n = sizes
    rest_n = hour_n * cat_n
    hour_own, rank = hour_factor.shape
    cat_own = cat_factor.shape[0]
    cells_here = demand.shape[2]

    own = jnp.concatenate(
        [
            jnp.pad(hour_factor, ((0, GROUP - hour_own), (0, 0))),
            jnp.pad(cat_factor, ((0, GROUP - cat_own), (0, 0))),
        ],
        axis=1,
    )
    own = call(rows_kernel, (cell_n, GROUP, LANES), BF16, (own,), 1000, 40000)
    rows = exchange(own, "cell", CELL_FIRST)
    message = call(
        functools.partial(partial_kernel, rank, hour_own, cat_own),
        (rest_n, SUMS + HOURS + 1, 2, LANES),
        BF16,
        (rows, demand),
        2 * rank * demand.size,
        2 * demand.size,
        [
            pltpu.VMEM((cell_n, GROUP, LANES), F32),
            pltpu.VMEM(demand.shape, BF16),
            pltpu.SemaphoreType.DMA((demand.shape[0] // STRIP,)),
        ],
        (1,),
        mib=50,
    )
    arrived = exchange(message, REST, REST_FIRST)
    summed = call(sum_kernel, (rest_n, TALL, LANES), BF16, (arrived,), 100000, 400000)
    gathered = exchange(summed, REST, REST_FIRST)
    inverse = call(
        functools.partial(inverse_kernel, rank), (3 * rank, LANES), BF16, (arrived,), 2**24, 10**7
    )
    return call(
        functools.partial(solve_kernel, rank),
        (rank, cells_here),
        F32,
        (inverse, gathered),
        6 * rank * rank * cells_here,
        400000,
        [pltpu.VMEM((rank, cells_here), F32), pltpu.SemaphoreType.DMA((cells_here // LANES // 2,))],
        (),
        True,
    )


def solution(mesh):
    sizes = tuple(mesh.shape[axis] for axis in ("cell", "hour", "cat"))
    in_specs = (P("hour", "cat", "cell"), P(("hour", "cell"), None), P(("cat", "cell"), None))
    out_specs = P(None, "cell")

    def body(demand, hour_factor, cat_factor):
        return shards(demand, hour_factor, cat_factor, sizes)

    return jax.shard_map(body, mesh=mesh, in_specs=in_specs, out_specs=out_specs, check_vma=False)
```

```python
import functools

import jax
import jax.numpy as jnp
from jax import lax
from jax.experimental import pallas as pl
from jax.experimental.pallas import tpu as pltpu
from jax.sharding import PartitionSpec as P

REST = ("hour", "cat")
LANES = 128
GROUP = 4
TALL = 16
SUMS = 8
HOURS = 4
F32 = jnp.float32
BF16 = jnp.bfloat16
CELL_FIRST = 10
REST_FIRST = 22
STRIP = 8


def iota(shape, dim):
    return lax.broadcasted_iota(jnp.int32, shape, dim)


def exchange(blocks, axes, first):
    order = [n ^ first for n in range(blocks.shape[0])]
    return lax.all_to_all(blocks, axes, 0, 0, axis_index_groups=[order])


def rows_kernel(own_ref, out_ref):
    out_ref[...] = jnp.broadcast_to(own_ref[...][None], out_ref.shape)


def partial_kernel(rank, hour_own, cat_own, rows_ref, demand_in, out_ref, groups_ref, demand_ref, sems):
    width = 256
    copies = []
    for n in range(demand_in.shape[0] // STRIP):
        part = pl.ds(n * STRIP, STRIP)
        copies.append(pltpu.make_async_copy(demand_in.at[part], demand_ref.at[part], sems.at[n]))
        copies[-1].start()
    cell_n = rows_ref.shape[0]
    hours_here, cats_here, cells_here = demand_ref.shape
    depth = hours_here * cats_here
    flat = rows_ref[...].astype(F32).reshape(cell_n * GROUP, LANES)
    groups_ref[...] = flat.reshape(cell_n, GROUP, LANES)
    turned = flat.T.astype(BF16)
    column = iota((cell_n * GROUP, depth), 1)
    row = iota((cell_n * GROUP, depth), 0)
    hour = column // cats_here
    pick_hour = (row == ((hour // hour_own) ^ CELL_FIRST) * GROUP + hour % hour_own).astype(F32).astype(BF16)
    cat = iota((cell_n * GROUP, LANES), 1) % cats_here
    cat_row = iota((cell_n * GROUP, LANES), 0)
    pick_cat = (cat_row == ((cat // cat_own) ^ CELL_FIRST) * GROUP + cat % cat_own).astype(F32).astype(BF16)
    hour_cols = jnp.dot(turned[:rank], pick_hour, preferred_element_type=F32)
    cat_cols = jnp.dot(turned[rank:], pick_cat, preferred_element_type=F32)
    cat_cols = jnp.concatenate([cat_cols] * (depth // LANES), axis=1)
    khatri = (hour_cols * cat_cols).astype(BF16)

    left_half = iota((2 * hour_own, LANES), 1) < rank
    hour_first = lax.axis_index("cat") * (TALL // hour_own)
    hours = [groups_ref[hour_first + step][:hour_own] for step in range(TALL // hour_own)]
    over = jnp.concatenate(hours[:2], axis=0)
    under = jnp.concatenate(hours[2:], axis=0)
    share = jnp.where(left_half, over, pltpu.roll(under, rank, 1)).astype(BF16)
    out_ref[:, SUMS : SUMS + HOURS] = jnp.broadcast_to(
        share.reshape(1, HOURS, 2, LANES), (out_ref.shape[0], HOURS, 2, LANES)
    )
    cat_first = lax.axis_index("hour") * 2
    both = jnp.concatenate([groups_ref[cat_first], groups_ref[cat_first + 1]], axis=0)
    over, under = pltpu.roll(both, rank, 1)[:cat_own], both[GROUP : GROUP + cat_own]
    share = jnp.where(left_half[:cat_own], over, under).astype(BF16)
    out_ref[:, SUMS + HOURS] = jnp.broadcast_to(share[None], (out_ref.shape[0], 2, LANES))

    across = cells_here // LANES
    chunk = STRIP * cats_here
    totals = [0.0] * (cells_here // width)
    for n, copy in enumerate(copies):
        copy.wait()
        columns = khatri[:, n * chunk : (n + 1) * chunk]
        for strip in range(len(totals)):
            block = demand_ref[n * STRIP : (n + 1) * STRIP, :, strip * width : (strip + 1) * width]
            totals[strip] += jnp.dot(columns, block.reshape(chunk, width), preferred_element_type=F32)
    for strip, total in enumerate(totals):
        left, sums = strip * width, total.astype(BF16)
        for down in range(rank // TALL):
            for over in range(width // LANES):
                piece = sums[down * TALL : (down + 1) * TALL, over * LANES : (over + 1) * LANES]
                out_ref[down * across + left // LANES + over, :SUMS] = piece.reshape(SUMS, 2, LANES)


def sum_kernel(arrived_ref, out_ref):
    count = arrived_ref.shape[0]
    terms = [arrived_ref[n, :SUMS].astype(F32) for n in range(count)]
    while len(terms) > 1:
        terms = [terms[n] + terms[n + 1] for n in range(0, len(terms), 2)]
    out_ref[...] = jnp.broadcast_to(terms[0].reshape(TALL, LANES).astype(BF16)[None], out_ref.shape)


def gram(pairs, rank):
    rows = pairs.astype(F32).reshape(-1, LANES).astype(BF16)
    both = lax.dot_general(rows, rows, (((0,), (0,)), ((), ())), preferred_element_type=F32)
    return both[:rank] + pltpu.roll(both[rank:], rank, 1)


def inverse_kernel(rank, arrived_ref, out_ref):
    normal = gram(arrived_ref[:, SUMS : SUMS + HOURS], rank) * gram(arrived_ref[:, SUMS + HOURS], rank)
    row, lane = iota((rank, LANES), 0), iota((rank, LANES), 1)
    diagonal = jnp.where(row == lane, normal, 0.0)
    by_row = lax.rsqrt(jnp.sum(diagonal, axis=1, keepdims=True))
    mirrored = diagonal + pltpu.roll(diagonal, rank, 1)
    by_lane = lax.rsqrt(jnp.sum(mirrored, axis=0, keepdims=True))
    left_half = lane < rank
    work = jnp.where(left_half, normal * by_row * by_lane, (row + rank == lane).astype(F32))
    blocks = [work[n * 8 : (n + 1) * 8] for n in range(rank // 8)]
    sub = iota((8, LANES), 0)
    for first in range(0, rank, 2):
        home, at = first // 8, first % 8
        columns_a = [jnp.broadcast_to(b[:, first : first + 1], (8, LANES)) for b in blocks]
        columns_b = [jnp.broadcast_to(b[:, first + 1 : first + 2], (8, LANES)) for b in blocks]
        row_a, row_b = blocks[home][at : at + 1], blocks[home][at + 1 : at + 2]
        p_aa, p_ba = columns_a[home][at : at + 1], columns_a[home][at + 1 : at + 2]
        p_ab, p_bb = columns_b[home][at : at + 1], columns_b[home][at + 1 : at + 2]
        scale = 1.0 / (p_aa * p_bb - p_ab * p_ba)
        new_a = (p_bb * row_a - p_ab * row_b) * scale
        new_b = (p_aa * row_b - p_ba * row_a) * scale
        new_a, new_b = jnp.broadcast_to(new_a, (8, LANES)), jnp.broadcast_to(new_b, (8, LANES))
        blocks = [b - (ca * new_a + cb * new_b) for b, ca, cb in zip(blocks, columns_a, columns_b)]
        blocks[home] = jnp.where(sub == at, new_a, jnp.where(sub == at + 1, new_b, blocks[home]))
    inverse = jnp.concatenate(blocks, axis=0) * by_row * by_lane
    inverse = pltpu.roll(inverse, rank, 1)
    high = inverse.astype(BF16)
    rest = inverse - high.astype(F32)
    middle = rest.astype(BF16)
    low = (rest - middle.astype(F32)).astype(BF16)
    out_ref[:rank] = high
    out_ref[rank : 2 * rank] = middle
    out_ref[2 * rank :] = low


def solve_kernel(rank, inverse_ref, sums_ref, out_hbm, out_ref, sems):
    copies = []
    cells_here = out_ref.shape[1]
    across = cells_here // LANES
    lhs = inverse_ref[...][:, :rank]
    for over in range(0, across, 2):
        rhs = jnp.concatenate(
            [
                jnp.concatenate([sums_ref[down * across + over + n] for down in range(rank // TALL)], axis=0)
                for n in range(2)
            ],
            axis=1,
        )
        terms = jnp.dot(lhs, rhs, preferred_element_type=F32)
        out_ref[:, over * LANES : (over + 2) * LANES] = terms[:rank] + (
            terms[rank : 2 * rank] + terms[2 * rank :]
        )
        part = pl.ds(over * LANES, 2 * LANES)
        copies.append(pltpu.make_async_copy(out_ref.at[:, part], out_hbm.at[:, part], sems.at[over // 2]))
        copies[-1].start()
    for copy in copies:
        copy.wait()


def call(kernel, shape, dtype, operands, flops, moved, scratch=(), left=(), leave_out=False, mib=24):
    vmem, anywhere = pl.BlockSpec(memory_space=pltpu.VMEM), pl.BlockSpec(memory_space=pltpu.HBM)
    return pl.pallas_call(
        kernel,
        out_shape=jax.ShapeDtypeStruct(shape, dtype),
        in_specs=[anywhere if n in left else vmem for n in range(len(operands))],
        out_specs=anywhere if leave_out else vmem,
        scratch_shapes=list(scratch),
        compiler_params=pltpu.CompilerParams(vmem_limit_bytes=mib * 1024 * 1024),
        cost_estimate=pl.CostEstimate(flops=flops, bytes_accessed=moved, transcendentals=0),
    )(*operands)


def shards(demand, hour_factor, cat_factor, sizes):
    cell_n, hour_n, cat_n = sizes
    rest_n = hour_n * cat_n
    hour_own, rank = hour_factor.shape
    cat_own = cat_factor.shape[0]
    cells_here = demand.shape[2]

    own = jnp.concatenate(
        [
            jnp.pad(hour_factor, ((0, GROUP - hour_own), (0, 0))),
            jnp.pad(cat_factor, ((0, GROUP - cat_own), (0, 0))),
        ],
        axis=1,
    ).reshape(GROUP // 2, 2, LANES)
    own = call(rows_kernel, (cell_n,) + own.shape, BF16, (own,), 1000, 40000)
    rows = exchange(own, "cell", CELL_FIRST)
    message = call(
        functools.partial(partial_kernel, rank, hour_own, cat_own),
        (rest_n, SUMS + HOURS + 1, 2, LANES),
        BF16,
        (rows, demand),
        2 * rank * demand.size,
        2 * demand.size,
        [
            pltpu.VMEM((cell_n, GROUP, LANES), F32),
            pltpu.VMEM(demand.shape, BF16),
            pltpu.SemaphoreType.DMA((demand.shape[0] // STRIP,)),
        ],
        (1,),
        mib=50,
    )
    arrived = exchange(message, REST, REST_FIRST)
    summed = call(sum_kernel, (rest_n, TALL, LANES), BF16, (arrived,), 100000, 400000)
    gathered = exchange(summed, REST, REST_FIRST)
    inverse = call(
        functools.partial(inverse_kernel, rank), (3 * rank, LANES), BF16, (arrived,), 2**24, 10**7
    )
    return call(
        functools.partial(solve_kernel, rank),
        (rank, cells_here),
        F32,
        (inverse, gathered),
        6 * rank * rank * cells_here,
        400000,
        [pltpu.VMEM((rank, cells_here), F32), pltpu.SemaphoreType.DMA((cells_here // LANES // 2,))],
        (),
        True,
    )


def solution(mesh):
    sizes = tuple(mesh.shape[axis] for axis in ("cell", "hour", "cat"))
    in_specs = (P("hour", "cat", "cell"), P(("hour", "cell"), None), P(("cat", "cell"), None))
    out_specs = P(None, "cell")

    def body(demand, hour_factor, cat_factor):
        return shards(demand, hour_factor, cat_factor, sizes)

    return jax.shard_map(body, mesh=mesh, in_specs=in_specs, out_specs=out_specs, check_vma=False)
```

```python
import functools

import jax
import jax.numpy as jnp
from jax import lax
from jax.experimental import pallas as pl
from jax.experimental.pallas import tpu as pltpu
from jax.sharding import PartitionSpec as P

REST = ("hour", "cat")
LANES = 128
GROUP = 4
TALL = 16
SUMS = 8
HOURS = 4
F32 = jnp.float32
BF16 = jnp.bfloat16
CELL_FIRST = 10
REST_FIRST = 22
STRIP = 8


def iota(shape, dim):
    return lax.broadcasted_iota(jnp.int32, shape, dim)


def exchange(blocks, axes, first):
    order = [n ^ first for n in range(blocks.shape[0])]
    return lax.all_to_all(blocks, axes, 0, 0, axis_index_groups=[order])


def rows_kernel(own_ref, out_ref):
    out_ref[...] = jnp.broadcast_to(own_ref[...][None], out_ref.shape)


def partial_kernel(rank, hour_own, cat_own, rows_ref, demand_in, out_ref, groups_ref, demand_ref, sems):
    width = 256
    copies = []
    for n in range(demand_in.shape[0] // STRIP):
        part = pl.ds(n * STRIP, STRIP)
        copies.append(pltpu.make_async_copy(demand_in.at[part], demand_ref.at[part], sems.at[n]))
        copies[-1].start()
    cell_n = rows_ref.shape[0]
    hours_here, cats_here, cells_here = demand_ref.shape
    depth = hours_here * cats_here
    flat = rows_ref[...].astype(F32).reshape(cell_n * GROUP, LANES)
    groups_ref[...] = flat.reshape(cell_n, GROUP, LANES)
    turned = flat.T.astype(BF16)
    column = iota((cell_n * GROUP, depth), 1)
    row = iota((cell_n * GROUP, depth), 0)
    hour = column // cats_here
    pick_hour = (row == ((hour // hour_own) ^ CELL_FIRST) * GROUP + hour % hour_own).astype(F32).astype(BF16)
    cat = iota((cell_n * GROUP, LANES), 1) % cats_here
    cat_row = iota((cell_n * GROUP, LANES), 0)
    pick_cat = (cat_row == ((cat // cat_own) ^ CELL_FIRST) * GROUP + cat % cat_own).astype(F32).astype(BF16)
    hour_cols = jnp.dot(turned[:rank], pick_hour, preferred_element_type=F32)
    cat_cols = jnp.dot(turned[rank:], pick_cat, preferred_element_type=F32)
    cat_cols = jnp.concatenate([cat_cols] * (depth // LANES), axis=1)
    khatri = (hour_cols * cat_cols).astype(BF16)

    left_half = iota((2 * hour_own, LANES), 1) < rank
    hour_first = lax.axis_index("cat") * (TALL // hour_own)
    hours = [groups_ref[hour_first + step][:hour_own] for step in range(TALL // hour_own)]
    over = jnp.concatenate(hours[:2], axis=0)
    under = jnp.concatenate(hours[2:], axis=0)
    share = jnp.where(left_half, over, pltpu.roll(under, rank, 1)).astype(BF16)
    out_ref[:, SUMS : SUMS + HOURS] = jnp.broadcast_to(
        share.reshape(1, HOURS, 2, LANES), (out_ref.shape[0], HOURS, 2, LANES)
    )
    cat_first = lax.axis_index("hour") * 2
    both = jnp.concatenate([groups_ref[cat_first], groups_ref[cat_first + 1]], axis=0)
    over, under = pltpu.roll(both, rank, 1)[:cat_own], both[GROUP : GROUP + cat_own]
    share = jnp.where(left_half[:cat_own], over, under).astype(BF16)
    out_ref[:, SUMS + HOURS] = jnp.broadcast_to(share[None], (out_ref.shape[0], 2, LANES))

    across = cells_here // LANES
    chunk = STRIP * cats_here
    totals = [0.0] * (cells_here // width)
    for n, copy in enumerate(copies):
        copy.wait()
        columns = khatri[:, n * chunk : (n + 1) * chunk]
        for strip in range(len(totals)):
            block = demand_ref[n * STRIP : (n + 1) * STRIP, :, strip * width : (strip + 1) * width]
            totals[strip] += jnp.dot(columns, block.reshape(chunk, width), preferred_element_type=F32)
    for strip, total in enumerate(totals):
        left, sums = strip * width, total.astype(BF16)
        for down in range(rank // TALL):
            for over in range(width // LANES):
                piece = sums[down * TALL : (down + 1) * TALL, over * LANES : (over + 1) * LANES]
                out_ref[down * across + left // LANES + over, :SUMS] = piece.reshape(SUMS, 2, LANES)


def sum_kernel(arrived_ref, out_hbm, block_ref, sems):
    count = arrived_ref.shape[0]
    terms = [arrived_ref[n, :SUMS].astype(F32) for n in range(count)]
    while len(terms) > 1:
        terms = [terms[n] + terms[n + 1] for n in range(0, len(terms), 2)]
    block_ref[...] = jnp.broadcast_to(terms[0].reshape(TALL, LANES).astype(BF16)[None], block_ref.shape)
    some = block_ref.shape[0]
    copies = [
        pltpu.make_async_copy(block_ref, out_hbm.at[pl.ds(n * some, some)], sems.at[n]) for n in range(count // some)
    ]
    for copy in copies:
        copy.start()
    for copy in copies:
        copy.wait()


def gram(pairs, rank):
    rows = pairs.astype(F32).reshape(-1, LANES).astype(BF16)
    both = lax.dot_general(rows, rows, (((0,), (0,)), ((), ())), preferred_element_type=F32)
    return both[:rank] + pltpu.roll(both[rank:], rank, 1)


def inverse_kernel(rank, arrived_ref, out_ref):
    normal = gram(arrived_ref[:, SUMS : SUMS + HOURS], rank) * gram(arrived_ref[:, SUMS + HOURS], rank)
    row, lane = iota((rank, LANES), 0), iota((rank, LANES), 1)
    diagonal = jnp.where(row == lane, normal, 0.0)
    by_row = lax.rsqrt(jnp.sum(diagonal, axis=1, keepdims=True))
    mirrored = diagonal + pltpu.roll(diagonal, rank, 1)
    by_lane = lax.rsqrt(jnp.sum(mirrored, axis=0, keepdims=True))
    left_half = lane < rank
    work = jnp.where(left_half, normal * by_row * by_lane, (row + rank == lane).astype(F32))
    blocks = [work[n * 8 : (n + 1) * 8] for n in range(rank // 8)]
    sub = iota((8, LANES), 0)
    for first in range(0, rank, 2):
        home, at = first // 8, first % 8
        columns_a = [jnp.broadcast_to(b[:, first : first + 1], (8, LANES)) for b in blocks]
        columns_b = [jnp.broadcast_to(b[:, first + 1 : first + 2], (8, LANES)) for b in blocks]
        row_a, row_b = blocks[home][at : at + 1], blocks[home][at + 1 : at + 2]
        p_aa, p_ba = columns_a[home][at : at + 1], columns_a[home][at + 1 : at + 2]
        p_ab, p_bb = columns_b[home][at : at + 1], columns_b[home][at + 1 : at + 2]
        scale = 1.0 / (p_aa * p_bb - p_ab * p_ba)
        new_a = (p_bb * row_a - p_ab * row_b) * scale
        new_b = (p_aa * row_b - p_ba * row_a) * scale
        new_a, new_b = jnp.broadcast_to(new_a, (8, LANES)), jnp.broadcast_to(new_b, (8, LANES))
        blocks = [b - (ca * new_a + cb * new_b) for b, ca, cb in zip(blocks, columns_a, columns_b)]
        blocks[home] = jnp.where(sub == at, new_a, jnp.where(sub == at + 1, new_b, blocks[home]))
    inverse = jnp.concatenate(blocks, axis=0) * by_row * by_lane
    inverse = pltpu.roll(inverse, rank, 1)
    high = inverse.astype(BF16)
    rest = inverse - high.astype(F32)
    middle = rest.astype(BF16)
    low = (rest - middle.astype(F32)).astype(BF16)
    out_ref[:rank] = high
    out_ref[rank : 2 * rank] = middle
    out_ref[2 * rank :] = low


def solve_kernel(rank, inverse_ref, sums_ref, out_hbm, out_ref, sems):
    copies = []
    cells_here = out_ref.shape[1]
    across = cells_here // LANES
    lhs = inverse_ref[...][:, :rank]
    for over in range(0, across, 2):
        rhs = jnp.concatenate(
            [
                jnp.concatenate([sums_ref[down * across + over + n] for down in range(rank // TALL)], axis=0)
                for n in range(2)
            ],
            axis=1,
        )
        terms = jnp.dot(lhs, rhs, preferred_element_type=F32)
        out_ref[:, over * LANES : (over + 2) * LANES] = terms[:rank] + (
            terms[rank : 2 * rank] + terms[2 * rank :]
        )
        part = pl.ds(over * LANES, 2 * LANES)
        copies.append(pltpu.make_async_copy(out_ref.at[:, part], out_hbm.at[:, part], sems.at[over // 2]))
        copies[-1].start()
    for copy in copies:
        copy.wait()


def call(kernel, shape, dtype, operands, flops, moved, scratch=(), left=(), leave_out=False, mib=24):
    vmem, anywhere = pl.BlockSpec(memory_space=pltpu.VMEM), pl.BlockSpec(memory_space=pltpu.HBM)
    return pl.pallas_call(
        kernel,
        out_shape=jax.ShapeDtypeStruct(shape, dtype),
        in_specs=[anywhere if n in left else vmem for n in range(len(operands))],
        out_specs=anywhere if leave_out else vmem,
        scratch_shapes=list(scratch),
        compiler_params=pltpu.CompilerParams(vmem_limit_bytes=mib * 1024 * 1024),
        cost_estimate=pl.CostEstimate(flops=flops, bytes_accessed=moved, transcendentals=0),
    )(*operands)


def shards(demand, hour_factor, cat_factor, sizes):
    cell_n, hour_n, cat_n = sizes
    rest_n = hour_n * cat_n
    hour_own, rank = hour_factor.shape
    cat_own = cat_factor.shape[0]
    cells_here = demand.shape[2]

    own = jnp.concatenate(
        [
            jnp.pad(hour_factor, ((0, GROUP - hour_own), (0, 0))),
            jnp.pad(cat_factor, ((0, GROUP - cat_own), (0, 0))),
        ],
        axis=1,
    ).reshape(GROUP // 2, 2, LANES)
    own = call(rows_kernel, (cell_n,) + own.shape, BF16, (own,), 1000, 40000)
    rows = exchange(own, "cell", CELL_FIRST)
    message = call(
        functools.partial(partial_kernel, rank, hour_own, cat_own),
        (rest_n, SUMS + HOURS + 1, 2, LANES),
        BF16,
        (rows, demand),
        2 * rank * demand.size,
        2 * demand.size,
        [
            pltpu.VMEM((cell_n, GROUP, LANES), F32),
            pltpu.VMEM(demand.shape, BF16),
            pltpu.SemaphoreType.DMA((demand.shape[0] // STRIP,)),
        ],
        (1,),
        mib=50,
    )
    arrived = exchange(message, REST, REST_FIRST)
    summed = call(
        sum_kernel,
        (rest_n, TALL, LANES),
        BF16,
        (arrived,),
        100000,
        400000,
        [pltpu.VMEM((rest_n // 4, TALL, LANES), BF16), pltpu.SemaphoreType.DMA((4,))],
        (),
        True,
    )
    gathered = exchange(summed, REST, REST_FIRST)
    inverse = call(
        functools.partial(inverse_kernel, rank), (3 * rank, LANES), BF16, (arrived,), 2**24, 10**7
    )
    return call(
        functools.partial(solve_kernel, rank),
        (rank, cells_here),
        F32,
        (inverse, gathered),
        6 * rank * rank * cells_here,
        400000,
        [pltpu.VMEM((rank, cells_here), F32), pltpu.SemaphoreType.DMA((cells_here // LANES // 2,))],
        (),
        True,
    )


def solution(mesh):
    sizes = tuple(mesh.shape[axis] for axis in ("cell", "hour", "cat"))
    in_specs = (P("hour", "cat", "cell"), P(("hour", "cell"), None), P(("cat", "cell"), None))
    out_specs = P(None, "cell")

    def body(demand, hour_factor, cat_factor):
        return shards(demand, hour_factor, cat_factor, sizes)

    return jax.shard_map(body, mesh=mesh, in_specs=in_specs, out_specs=out_specs, check_vma=False)
```
